32 devices in a mesh: groups: 2 (over y), expert: 16 (over z, x, core), sub: 1.
Axes of the slice: x: 2, y: 2, z: 4, core: 2. Of those that a mesh axis runs over, the one named last changes fastest.
Arguments:
- gate_up: bfloat16 [512, 8, 2, 1024], P(('groups', 'expert', 'sub')), parts along dimension 0, may hold values from -8 to 8
- routes: int32 [512, 8], P(('groups', 'expert', 'sub')), parts along dimension 0, may hold values from 0 to 15, all different within a row; in each aligned block of 16 rows (0 to 15, 16 to 31, ...) at most 16 rows name the same one
Outputs:
- gram: float32 [32, 1024, 1024], P(('groups', 'expert'), 'sub'), parts along dimension 0
The draws below stay inside these ranges and needn't reach their ends.
There are 2 independent parts, one for each index of `groups`. The reference program is written for one: setup_inputs(seed, part) draws one part's arguments, and reference() takes and returns one part's arrays. A program takes and returns all parts, laid end to end along the dimension named above; each array names one. Nothing has to cross between parts.
Inputs may be any that keep to these rules, and one draw needn't show every extreme that they name: `routes`: each token names 8 different experts; among the tokens of one device no expert is named more than 16 times, a bound that some block reaches; every expert is named somewhere.
All inputs are finite; a program needn't handle non-finite values.
Results may differ from the reference program's by a relative error of at most 0.0038.
Values may be sent and summed in bfloat16 or wider, within the bound.
A program may use at most 64 MiB of HBM per device.

```python
import math
import jax
import jax.numpy as jnp
import numpy as np
from jax import lax

FF = 1024
TOP = 8
TOK_DEV = 16
EXPERTS = 16
TOKENS = 256
CAP = 16
MEAN_ROWS = 128
N_EXPERT = 16
N_SUB = 1


def levels(rng, shape, shards, smallest, top_value):
    level, own = 1.0, jax.random.fold_in(rng, 6)
    for position, parts in shards:
        draws = jnp.exp(jax.random.uniform(jax.random.fold_in(own, position), (parts,), jnp.float32, smallest / len(shards), top_value / len(shards)))
        level = level * jnp.repeat(draws, shape[position] // parts).reshape([-1 if axis == position else 1 for axis in range(len(shape))])
    return level


def assign_block(stream_key, own, number, rows, amount, top, bound, lean):
    sequence = jax.random.permutation(stream_key, amount)
    crowded, ordinary = portions_of(amount, rows * top, bound, lean, True), portions_of(amount, rows * top, bound, lean, False)
    places = jnp.arange(amount)

    def named(sizes, rotation):
        used = int((sizes > 0).sum())
        fixed = max(1, used // 4)
        shifted = fixed + (places - fixed + rotation * (used - fixed)) % max(1, amount - fixed)
        return jnp.zeros((amount,), jnp.int32).at[sequence[jnp.where(places < fixed, places, shifted)]].set(jnp.asarray(sizes, jnp.int32))

    sizes = jnp.where(number % 4 == 0, named(crowded, number // 4), named(ordinary, number - number // 4 - 1))
    mixed = jax.random.permutation(jax.random.fold_in(own, 3), amount)
    source_of, sink = mixed[0:amount // 2 * 2:2], mixed[1:amount // 2 * 2:2]
    room = jnp.minimum(sizes[source_of] - 1, bound - sizes[sink]) // 2
    room = jnp.where((source_of == sequence[0]) | (sink == sequence[0]) | (sizes[sink] == 0), 0, jnp.maximum(room, 0))
    shifted = jax.random.randint(jax.random.fold_in(own, 4), (amount // 2,), 0, 1 << 20) % (room + 1)
    sizes = sizes.at[source_of].add(-shifted).at[sink].add(shifted)
    items = jnp.searchsorted(jnp.cumsum(sizes), jnp.arange(rows * top), side="right").astype(jnp.int32)
    grid = items.reshape(top, rows).T
    grid = grid[jax.random.permutation(jax.random.fold_in(own, 1), rows)]
    rotation = jax.random.randint(jax.random.fold_in(own, 2), (rows, 1), 0, top)
    return jnp.take_along_axis(grid, (jnp.arange(top)[None, :] + rotation) % top, axis=1)


def portions_of(number_of, total, reach, skew, full):
    portions = [(1 << 20) // math.isqrt(rank ** skew) + 1 for rank in range(1, number_of + 1)]
    largest = reach if full else min(reach, max(-(-total // number_of), total * portions[0] // sum(portions)))
    least = 1 if total - largest >= number_of - 1 else 0
    holding, rest = [largest] + [least] * (number_of - 1), total - largest - least * (number_of - 1)
    while rest > 0:
        candidates = [i for i in range(1, number_of) if holding[i] < largest] or [i for i in range(1, number_of) if holding[i] < reach]
        whole, budget = sum([portions[i] for i in candidates]), rest
        for i in candidates:
            more = min(reach - holding[i], max(1, budget * portions[i] // whole), rest)
            holding[i] = holding[i] + more
            rest = rest - more
    return np.array(holding)


def noise(key, shape, width, reach, pieces=(), kind=jnp.bfloat16):
    values = width * jax.random.normal(key, shape, jnp.float32)
    if pieces:
        values = values * levels(key, shape, pieces, -0.22, 0.18)
    return jnp.clip(values, -reach, reach).astype(kind)


def setup_inputs(seed: int = 0, part: int = 0) -> dict:
    splits = jax.random.split(jax.random.key(seed), 3)
    part_keys = jax.random.split(jax.random.fold_in(splits[2], part), 3)
    gate_up = noise(part_keys[0], (TOKENS, TOP, 2, FF), 1.5, 8.0, ((0, 16),))
    routes_keys = jax.random.split(jax.random.fold_in(part_keys[1], 1), TOKENS // TOK_DEV)
    routes_turns = jax.random.permutation(jax.random.fold_in(part_keys[1], 3), TOKENS // TOK_DEV)
    routes = jax.vmap(lambda own, number: assign_block(jax.random.fold_in(part_keys[1], 2), own, number, TOK_DEV, EXPERTS, TOP, CAP, 2))(routes_keys, routes_turns).reshape((TOKENS, TOP))
    return {"gate_up": gate_up, "routes": routes}


def reference(gate_up, routes):
    gate = gate_up[:, :, 0, :].astype(jnp.float32)
    upper = gate_up[:, :, 1, :].astype(jnp.float32)
    hidden = (jax.nn.silu(gate) * upper).astype(jnp.bfloat16)
    hidden = hidden.reshape(TOKENS * TOP, FF)
    flat = routes.reshape(-1).astype(jnp.int32)
    order = jnp.argsort(flat, stable=True).astype(jnp.int32)
    most = N_EXPERT * N_SUB * CAP
    ordered = jnp.concatenate([hidden[order], jnp.zeros((most, FF), hidden.dtype)], axis=0)
    counts = jnp.sum((flat[:, None] == jnp.arange(EXPERTS, dtype=jnp.int32)[None, :]).astype(jnp.int32), axis=0)
    offsets = (jnp.cumsum(counts) - counts).astype(jnp.int32)

    def one_expert(expert):
        start = offsets[expert].astype(jnp.int32)
        block = lax.dynamic_slice_in_dim(ordered, start, most, 0)
        keep = (jnp.arange(most, dtype=jnp.int32) < counts[expert])[:, None]
        block = jnp.where(keep, block, jnp.zeros_like(block))
        return jnp.dot(block.T, block, preferred_element_type=jnp.float32)

    gram = lax.map(one_expert, jnp.arange(EXPERTS, dtype=jnp.int32))
    return gram * (1.0 / MEAN_ROWS)
```

```python
import functools

import jax
import jax.numpy as jnp
from jax import lax
from jax.experimental import pallas as pl
from jax.experimental.pallas import tpu as pltpu
from jax.sharding import PartitionSpec as P

MESH = pl.DeviceIdType.MESH


def hidden_rows(gate_up):
    gate = gate_up[..., 0, :].astype(jnp.float32)
    upper = gate_up[..., 1, :].astype(jnp.float32)
    return (jax.nn.silu(gate) * upper).astype(jnp.bfloat16)


def partner(me, owners, step):
    half = owners // 2
    mine, place = me // half, me % half
    far = (1 - mine) * half + (place + step) % half
    near = mine * half + (place + step + 1 - half) % half
    return jnp.where(step < half, far, near)


def exchange_kernel(owners, tok_rows, picks, hidden_ref, routes_ref, got_ref, send_ref, send_sem, recv_sem):
    me = lax.axis_index("expert")
    half = owners // 2
    mine, place = me // half, me % half

    def peer(step):
        if step < half:
            return (1 - mine) * half + (place + step) % half
        return mine * half + (place + step + 1 - half) % half

    barrier = pltpu.get_barrier_semaphore()
    for step in range(owners - 1):
        pl.semaphore_signal(barrier, inc=1, device_id={"expert": peer(step)}, device_id_type=MESH)

    entries = tok_rows * picks
    token = lax.broadcasted_iota(jnp.int32, (tok_rows, entries), 0)
    entry = lax.broadcasted_iota(jnp.int32, (tok_rows, entries), 1)
    spread = (entry // picks == token).astype(jnp.float32)
    by_pick = jnp.dot(routes_ref[...].astype(jnp.float32), spread, preferred_element_type=jnp.float32)
    pick = lax.broadcasted_iota(jnp.int32, (picks, entries), 0)
    entry = lax.broadcasted_iota(jnp.int32, (picks, entries), 1)
    flat = jnp.sum(jnp.where(entry % picks == pick, by_pick, 0.0), axis=0, keepdims=True).astype(jnp.int32)

    rows = owners * tok_rows
    row = lax.broadcasted_iota(jnp.int32, (rows, entries), 0)
    entry = lax.broadcasted_iota(jnp.int32, (rows, entries), 1)
    named = partner(me, owners, row // tok_rows)
    choose = jnp.where((flat == named) & (entry // picks == row % tok_rows), 1.0, 0.0).astype(jnp.bfloat16)
    placed = jnp.dot(choose, hidden_ref[...], preferred_element_type=jnp.float32).astype(jnp.bfloat16)
    last = rows - tok_rows
    send_ref[...] = placed[:last]
    got_ref[last:, :] = placed[last:]

    pl.semaphore_wait(barrier, owners - 1)
    copies = []
    for step in range(owners - 1):
        block = pl.ds(step * tok_rows, tok_rows)
        copy = pltpu.make_async_remote_copy(
            src_ref=send_ref.at[block],
            dst_ref=got_ref.at[block],
            send_sem=send_sem.at[step],
            recv_sem=recv_sem.at[step],
            device_id={"expert": peer(step)},
            device_id_type=MESH,
        )
        copy.start()
        copies.append(copy)
    for copy in copies:
        copy.wait()


def exchange(hidden, routes, owners):
    entries, width = hidden.shape
    picks, tok_rows = routes.shape
    rows = owners * tok_rows
    return pl.pallas_call(
        functools.partial(exchange_kernel, owners, tok_rows, picks),
        out_shape=jax.ShapeDtypeStruct((rows, width), jnp.bfloat16),
        in_specs=[pl.BlockSpec(memory_space=pltpu.VMEM)] * 2,
        out_specs=pl.BlockSpec(memory_space=pltpu.VMEM),
        scratch_shapes=[
            pltpu.VMEM((rows - tok_rows, width), jnp.bfloat16),
            pltpu.SemaphoreType.DMA((owners - 1,)),
            pltpu.SemaphoreType.DMA((owners - 1,)),
        ],
        compiler_params=pltpu.CompilerParams(
            collective_id=0, has_side_effects=True, vmem_limit_bytes=16 * 1024 * 1024
        ),
    )(hidden, routes)


def exchange_plain(hidden, routes, owners, capacity):
    entries, width = hidden.shape
    flat = routes.reshape(-1)
    onehot = (flat[:, None] == jnp.arange(owners, dtype=jnp.int32)[None, :]).astype(jnp.int32)
    ranks = jnp.sum(jnp.cumsum(onehot, axis=0) * onehot, axis=1) - 1
    slots = flat * capacity + ranks
    choose = (jnp.arange(owners * capacity, dtype=jnp.int32)[:, None] == slots[None, :]).astype(jnp.bfloat16)
    send = jnp.dot(choose, hidden, preferred_element_type=jnp.float32).astype(jnp.bfloat16)
    send = send.reshape(owners, capacity, width)
    return lax.all_to_all(send, "expert", split_axis=0, concat_axis=0, tiled=True).reshape(owners * capacity, width)


def per_device(gate_up, routes):
    tok_rows, picks, _, width = gate_up.shape
    owners = lax.axis_size("expert")
    halves = lax.axis_size("sub")
    capacity = max(2, min(tok_rows, 2 * tok_rows * picks // owners))
    scale = 1.0 / (tok_rows * picks * halves)
    hidden = hidden_rows(gate_up).reshape(tok_rows * picks, width)
    if capacity == tok_rows and tok_rows % 16 == 0 and owners % 2 == 0 and owners <= 32 and halves == 1:
        rows = exchange(hidden, routes.T, owners)
        gram = jnp.einsum("rc,rd->cd", rows, rows, preferred_element_type=jnp.float32)
    else:
        rows = exchange_plain(hidden, routes, owners, capacity)
        gram = jnp.einsum("rc,rd->cd", rows, rows, preferred_element_type=jnp.float32)
        if halves > 1:
            gram = lax.psum_scatter(gram, "sub", scatter_dimension=0, tiled=True)
    return (gram * scale)[None]


def solution(mesh):
    placed = (
        P(("groups", "expert", "sub"), None, None, None),
        P(("groups", "expert", "sub"), None),
    )
    return jax.shard_map(
        per_device,
        mesh=mesh,
        in_specs=placed,
        out_specs=P(("groups", "expert"), "sub", None),
        check_vma=False,
    )
```

```python
import functools

import jax
import jax.numpy as jnp
from jax import lax
from jax.experimental import pallas as pl
from jax.experimental.pallas import tpu as pltpu
from jax.sharding import PartitionSpec as P

MESH = pl.DeviceIdType.MESH


def hidden_rows(gate_up):
    gate = gate_up[..., 0, :].astype(jnp.float32)
    upper = gate_up[..., 1, :].astype(jnp.float32)
    return (jax.nn.silu(gate) * upper).astype(jnp.bfloat16)


def partner(me, owners, quarter, step):
    half = owners // 2
    mine, plane, place = me // half, me // quarter, me % quarter
    group, turn = step // quarter, step % quarter
    if isinstance(step, int):
        plane_to = [(1 - mine) * 2, (1 - mine) * 2 + 1, mine * 2 + 1 - plane % 2, plane][group]
    else:
        plane_to = jnp.where(group < 2, (1 - mine) * 2 + group, jnp.where(group == 2, mine * 2 + 1 - plane % 2, plane))
    return plane_to * quarter + (place + turn + group // 3) % quarter


def exchange_kernel(
    owners, gate_up_ref, routes_ref, got_ref, raw_ref, named_ref, hidden_ref, send_ref, in_sem, send_sem, recv_sem
):
    me = lax.axis_index("expert")
    entries, _, width = gate_up_ref.shape
    picks, tok_rows = routes_ref.shape
    quarter = owners // 4
    pieces = in_sem.shape[0] - 1

    barrier = pltpu.get_barrier_semaphore()
    for step in range(owners - 1):
        pl.semaphore_signal(
            barrier, inc=1, device_id={"expert": partner(me, owners, quarter, step)}, device_id_type=MESH
        )

    routes_in = pltpu.make_async_copy(routes_ref, named_ref, in_sem.at[pieces])
    routes_in.start()
    part = entries // pieces
    loads = []
    for piece in range(pieces):
        span = pl.ds(piece * part, part)
        loads.append(pltpu.make_async_copy(gate_up_ref.at[span], raw_ref.at[span], in_sem.at[piece]))
        loads[-1].start()

    routes_in.wait()
    token = lax.broadcasted_iota(jnp.int32, (tok_rows, entries), 0)
    entry = lax.broadcasted_iota(jnp.int32, (tok_rows, entries), 1)
    spread = (entry // picks == token).astype(jnp.float32)
    by_pick = jnp.dot(named_ref[...].astype(jnp.float32), spread, preferred_element_type=jnp.float32)
    pick = lax.broadcasted_iota(jnp.int32, (picks, entries), 0)
    entry = lax.broadcasted_iota(jnp.int32, (picks, entries), 1)
    flat = jnp.sum(jnp.where(entry % picks == pick, by_pick, 0.0), axis=0, keepdims=True).astype(jnp.int32)

    rows = owners * tok_rows
    row = lax.broadcasted_iota(jnp.int32, (rows, 1), 0)
    goes_to = partner(me, owners, quarter, row // tok_rows)
    entry = lax.broadcasted_iota(jnp.int32, (rows, entries), 1)
    choose = jnp.where((flat == goes_to) & (entry // picks == row % tok_rows), 1.0, 0.0).astype(jnp.bfloat16)

    for piece in range(pieces):
        loads[piece].wait()
        span = pl.ds(piece * part, part)
        both = raw_ref[span].reshape(part, 2 * width)
        gate = both[:, :width].astype(jnp.float32)
        upper = both[:, width:].astype(jnp.float32)
        hidden_ref[span] = (jax.nn.silu(gate) * upper).astype(jnp.bfloat16)

    def place(first, count):
        picked = choose[first : first + count]
        return jnp.dot(picked, hidden_ref[...], preferred_element_type=jnp.float32).astype(jnp.bfloat16)

    middle, last = rows // 2, rows - tok_rows
    send_ref[:middle] = place(0, middle)
    pl.semaphore_wait(barrier, owners - 1)
    parity = (me // quarter) % 2

    def exchanged(step, slot):
        return pltpu.make_async_remote_copy(
            src_ref=send_ref.at[pl.ds(step * tok_rows, tok_rows)],
            dst_ref=got_ref.at[pl.ds(pl.multiple_of(slot * tok_rows, tok_rows), tok_rows)],
            send_sem=send_sem.at[step],
            recv_sem=recv_sem.at[slot],
            device_id={"expert": partner(me, owners, quarter, step)},
            device_id_type=MESH,
        )

    def send(step):
        slot = parity * quarter + step % quarter if step < owners // 2 else step
        exchanged(step, slot).start()

    for step in range(owners // 2):
        send(step)
    rest = place(middle, middle)
    send_ref[middle:] = rest[: last - middle]
    got_ref[last:, :] = rest[last - middle :]
    for step in range(owners // 2, owners - 1):
        send(step)
    for step in range(owners - 1):
        exchanged(step, step).wait()


def exchange(gate_up, routes, owners):
    entries, _, width = gate_up.shape
    picks, tok_rows = routes.shape
    rows = owners * tok_rows
    pieces = 4
    return pl.pallas_call(
        functools.partial(exchange_kernel, owners),
        out_shape=jax.ShapeDtypeStruct((rows, width), jnp.bfloat16),
        in_specs=[pl.BlockSpec(memory_space=pltpu.HBM)] * 2,
        out_specs=pl.BlockSpec(memory_space=pltpu.VMEM),
        scratch_shapes=[
            pltpu.VMEM((entries, 2, width), jnp.bfloat16),
            pltpu.VMEM((picks, tok_rows), jnp.int32),
            pltpu.VMEM((entries, width), jnp.bfloat16),
            pltpu.VMEM((rows - tok_rows, width), jnp.bfloat16),
            pltpu.SemaphoreType.DMA((pieces + 1,)),
            pltpu.SemaphoreType.DMA((owners - 1,)),
            pltpu.SemaphoreType.DMA((owners - 1,)),
        ],
        compiler_params=pltpu.CompilerParams(
            collective_id=0, has_side_effects=True, vmem_limit_bytes=54400 * 1024
        ),
    )(gate_up, routes)


def gram_kernel(scale, tiles, rows_ref, gram_ref, tile_ref, out_sem):
    width = rows_ref.shape[1]
    height = width // tiles
    writes = []
    for tile in range(tiles):
        span = pl.ds(tile * height, height)
        product = lax.dot_general(
            rows_ref[:, span], rows_ref[...], (((0,), (0,)), ((), ())), preferred_element_type=jnp.float32
        )
        tile_ref[span] = product * scale
        writes.append(pltpu.make_async_copy(tile_ref.at[span], gram_ref.at[span], out_sem.at[tile]))
        writes[-1].start()
    for write in writes:
        write.wait()


def gram_of(rows, scale):
    width = rows.shape[1]
    tiles = 8 if width % 1024 == 0 else 1
    return pl.pallas_call(
        functools.partial(gram_kernel, scale, tiles),
        out_shape=jax.ShapeDtypeStruct((width, width), jnp.float32),
        in_specs=[pl.BlockSpec(memory_space=pltpu.VMEM)],
        out_specs=pl.BlockSpec(memory_space=pltpu.HBM),
        scratch_shapes=[pltpu.VMEM((width, width), jnp.float32), pltpu.SemaphoreType.DMA((tiles,))],
        compiler_params=pltpu.CompilerParams(vmem_limit_bytes=32 * 1024 * 1024),
    )(rows)


def exchange_plain(hidden, routes, owners, capacity):
    entries, width = hidden.shape
    flat = routes.reshape(-1)
    onehot = (flat[:, None] == jnp.arange(owners, dtype=jnp.int32)[None, :]).astype(jnp.int32)
    ranks = jnp.sum(jnp.cumsum(onehot, axis=0) * onehot, axis=1) - 1
    slots = flat * capacity + ranks
    choose = (jnp.arange(owners * capacity, dtype=jnp.int32)[:, None] == slots[None, :]).astype(jnp.bfloat16)
    send = jnp.dot(choose, hidden, preferred_element_type=jnp.float32).astype(jnp.bfloat16)
    send = send.reshape(owners, capacity, width)
    return lax.all_to_all(send, "expert", split_axis=0, concat_axis=0, tiled=True).reshape(owners * capacity, width)


def per_device(gate_up, routes):
    tok_rows, picks, _, width = gate_up.shape
    owners = lax.axis_size("expert")
    halves = lax.axis_size("sub")
    capacity = max(2, min(tok_rows, 2 * tok_rows * picks // owners))
    scale = 1.0 / (tok_rows * picks * halves)
    if capacity == tok_rows and tok_rows % 16 == 0 and owners % 4 == 0 and owners <= 32 and halves == 1:
        rows = exchange(gate_up.reshape(tok_rows * picks, 2, width), routes.T, owners)
        return gram_of(rows, scale)[None]
    hidden = hidden_rows(gate_up).reshape(tok_rows * picks, width)
    rows = exchange_plain(hidden, routes, owners, capacity)
    gram = jnp.einsum("rc,rd->cd", rows, rows, preferred_element_type=jnp.float32)
    gram = lax.psum_scatter(gram, "sub", scatter_dimension=0, tiled=True)
    return (gram * scale)[None]


def solution(mesh):
    placed = (
        P(("groups", "expert", "sub"), None, None, None),
        P(("groups", "expert", "sub"), None),
    )
    return jax.shard_map(
        per_device,
        mesh=mesh,
        in_specs=placed,
        out_specs=P(("groups", "expert"), "sub", None),
        check_vma=False,
    )
```

```python
import functools

import jax
import jax.numpy as jnp
from jax import lax
from jax.experimental import pallas as pl
from jax.experimental.pallas import tpu as pltpu
from jax.sharding import PartitionSpec as P

MESH = pl.DeviceIdType.MESH


def hidden_rows(gate_up):
    gate = gate_up[..., 0, :].astype(jnp.float32)
    upper = gate_up[..., 1, :].astype(jnp.float32)
    return (jax.nn.silu(gate) * upper).astype(jnp.bfloat16)


def partner(me, owners, quarter, step):
    half = owners // 2
    mine, plane, place = me // half, me // quarter, me % quarter
    group, turn = step // quarter, step % quarter
    if isinstance(step, int):
        plane_to = [(1 - mine) * 2, (1 - mine) * 2 + 1, mine * 2 + 1 - plane % 2, plane][group]
    else:
        plane_to = jnp.where(group < 2, (1 - mine) * 2 + group, jnp.where(group == 2, mine * 2 + 1 - plane % 2, plane))
    return plane_to * quarter + (place + turn + group // 3) % quarter


def exchange_kernel(
    owners, gate_up_ref, routes_ref, got_ref, raw_ref, named_ref, hidden_ref, send_ref, in_sem, send_sem, recv_sem
):
    me = lax.axis_index("expert")
    entries, _, width = gate_up_ref.shape
    picks, tok_rows = routes_ref.shape
    quarter = owners // 4
    pieces = in_sem.shape[0] - 1

    barrier = pltpu.get_barrier_semaphore()
    for step in range(owners - 1):
        pl.semaphore_signal(
            barrier, inc=1, device_id={"expert": partner(me, owners, quarter, step)}, device_id_type=MESH
        )

    routes_in = pltpu.make_async_copy(routes_ref, named_ref, in_sem.at[pieces])
    routes_in.start()
    part = entries // pieces
    loads = []
    for piece in range(pieces):
        span = pl.ds(piece * part, part)
        loads.append(pltpu.make_async_copy(gate_up_ref.at[span], raw_ref.at[span], in_sem.at[piece]))
        loads[-1].start()

    routes_in.wait()
    token = lax.broadcasted_iota(jnp.int32, (tok_rows, entries), 0)
    entry = lax.broadcasted_iota(jnp.int32, (tok_rows, entries), 1)
    spread = (entry // picks == token).astype(jnp.float32)
    by_pick = jnp.dot(named_ref[...].astype(jnp.float32), spread, preferred_element_type=jnp.float32)
    pick = lax.broadcasted_iota(jnp.int32, (picks, entries), 0)
    entry = lax.broadcasted_iota(jnp.int32, (picks, entries), 1)
    flat = jnp.sum(jnp.where(entry % picks == pick, by_pick, 0.0), axis=0, keepdims=True).astype(jnp.int32)

    rows = owners * tok_rows
    row = lax.broadcasted_iota(jnp.int32, (rows, 1), 0)
    goes_to = partner(me, owners, quarter, row // tok_rows)
    entry = lax.broadcasted_iota(jnp.int32, (rows, entries), 1)
    choose = jnp.where((flat == goes_to) & (entry // picks == row % tok_rows), 1.0, 0.0).astype(jnp.bfloat16)

    for piece in range(pieces):
        loads[piece].wait()
        span = pl.ds(piece * part, part)
        both = raw_ref[span].reshape(part, 2 * width)
        gate = both[:, :width].astype(jnp.float32)
        upper = both[:, width:].astype(jnp.float32)
        hidden_ref[span] = (jax.nn.silu(gate) * upper).astype(jnp.bfloat16)

    def place(first, count):
        picked = choose[first : first + count]
        return jnp.dot(picked, hidden_ref[...], preferred_element_type=jnp.float32).astype(jnp.bfloat16)

    middle, last = rows // 2, rows - tok_rows
    send_ref[:middle] = place(0, middle)
    pl.semaphore_wait(barrier, owners - 1)
    parity = (me // quarter) % 2

    def exchanged(step, slot):
        return pltpu.make_async_remote_copy(
            src_ref=send_ref.at[pl.ds(step * tok_rows, tok_rows)],
            dst_ref=got_ref.at[pl.ds(pl.multiple_of(slot * tok_rows, tok_rows), tok_rows)],
            send_sem=send_sem.at[step],
            recv_sem=recv_sem.at[slot],
            device_id={"expert": partner(me, owners, quarter, step)},
            device_id_type=MESH,
        )

    def send(step):
        slot = parity * quarter + step % quarter if step < owners // 2 else step
        exchanged(step, slot).start()

    for step in range(owners // 2):
        send(step)
    rest = place(middle, middle)
    send_ref[middle:] = rest[: last - middle]
    got_ref[last:, :] = rest[last - middle :]
    for step in range(owners // 2, owners - 1):
        send(step)
    for step in range(owners - 1):
        exchanged(step, step).wait()


def exchange(gate_up, routes, owners):
    entries, _, width = gate_up.shape
    picks, tok_rows = routes.shape
    rows = owners * tok_rows
    pieces = 4
    return pl.pallas_call(
        functools.partial(exchange_kernel, owners),
        out_shape=jax.ShapeDtypeStruct((rows, width), jnp.bfloat16),
        in_specs=[pl.BlockSpec(memory_space=pltpu.HBM)] * 2,
        out_specs=pl.BlockSpec(memory_space=pltpu.VMEM),
        scratch_shapes=[
            pltpu.VMEM((entries, 2, width), jnp.bfloat16),
            pltpu.VMEM((picks, tok_rows), jnp.int32),
            pltpu.VMEM((entries, width), jnp.bfloat16),
            pltpu.VMEM((rows - tok_rows, width), jnp.bfloat16),
            pltpu.SemaphoreType.DMA((pieces + 1,)),
            pltpu.SemaphoreType.DMA((owners - 1,)),
            pltpu.SemaphoreType.DMA((owners - 1,)),
        ],
        compiler_params=pltpu.CompilerParams(
            collective_id=0, has_side_effects=True, vmem_limit_bytes=32 * 1024 * 1024
        ),
    )(pltpu.with_memory_space_constraint(gate_up, pltpu.HBM), pltpu.with_memory_space_constraint(routes, pltpu.HBM))


def gram_kernel(scale, tiles, rows_ref, gram_ref, tile_ref, out_sem):
    width = rows_ref.shape[1]
    height = width // tiles
    writes = []
    for tile in range(tiles):
        span = pl.ds(tile * height, height)
        product = lax.dot_general(
            rows_ref[:, span], rows_ref[...], (((0,), (0,)), ((), ())), preferred_element_type=jnp.float32
        )
        tile_ref[span] = product * scale
        writes.append(pltpu.make_async_copy(tile_ref.at[span], gram_ref.at[span], out_sem.at[tile]))
        writes[-1].start()
    for write in writes:
        write.wait()


def gram_of(rows, scale):
    width = rows.shape[1]
    tiles = 8 if width % 1024 == 0 else 1
    return pl.pallas_call(
        functools.partial(gram_kernel, scale, tiles),
        out_shape=jax.ShapeDtypeStruct((width, width), jnp.float32),
        in_specs=[pl.BlockSpec(memory_space=pltpu.VMEM)],
        out_specs=pl.BlockSpec(memory_space=pltpu.HBM),
        scratch_shapes=[pltpu.VMEM((width, width), jnp.float32), pltpu.SemaphoreType.DMA((tiles,))],
        compiler_params=pltpu.CompilerParams(vmem_limit_bytes=32 * 1024 * 1024),
    )(rows)


def exchange_plain(hidden, routes, owners, capacity):
    entries, width = hidden.shape
    flat = routes.reshape(-1)
    onehot = (flat[:, None] == jnp.arange(owners, dtype=jnp.int32)[None, :]).astype(jnp.int32)
    ranks = jnp.sum(jnp.cumsum(onehot, axis=0) * onehot, axis=1) - 1
    slots = flat * capacity + ranks
    choose = (jnp.arange(owners * capacity, dtype=jnp.int32)[:, None] == slots[None, :]).astype(jnp.bfloat16)
    send = jnp.dot(choose, hidden, preferred_element_type=jnp.float32).astype(jnp.bfloat16)
    send = send.reshape(owners, capacity, width)
    return lax.all_to_all(send, "expert", split_axis=0, concat_axis=0, tiled=True).reshape(owners * capacity, width)


def per_device(gate_up, routes):
    tok_rows, picks, _, width = gate_up.shape
    owners = lax.axis_size("expert")
    halves = lax.axis_size("sub")
    capacity = max(2, min(tok_rows, 2 * tok_rows * picks // owners))
    scale = 1.0 / (tok_rows * picks * halves)
    if capacity == tok_rows and tok_rows % 16 == 0 and owners % 4 == 0 and owners <= 32 and halves == 1:
        rows = exchange(gate_up.reshape(tok_rows * picks, 2, width), routes.T, owners)
        return gram_of(rows, scale)[None]
    hidden = hidden_rows(gate_up).reshape(tok_rows * picks, width)
    rows = exchange_plain(hidden, routes, owners, capacity)
    gram = jnp.einsum("rc,rd->cd", rows, rows, preferred_element_type=jnp.float32)
    gram = lax.psum_scatter(gram, "sub", scatter_dimension=0, tiled=True)
    return (gram * scale)[None]


def solution(mesh):
    placed = (
        P(("groups", "expert", "sub"), None, None, None),
        P(("groups", "expert", "sub"), None),
    )
    return jax.shard_map(
        per_device,
        mesh=mesh,
        in_specs=placed,
        out_specs=P(("groups", "expert"), "sub", None),
        check_vma=False,
    )
```

```python
import functools

import jax
import jax.numpy as jnp
from jax import lax
from jax.experimental import pallas as pl
from jax.experimental.pallas import tpu as pltpu
from jax.sharding import PartitionSpec as P

MESH = pl.DeviceIdType.MESH


def hidden_rows(gate_up):
    gate = gate_up[..., 0, :].astype(jnp.float32)
    upper = gate_up[..., 1, :].astype(jnp.float32)
    return (jax.nn.silu(gate) * upper).astype(jnp.bfloat16)


def partner(me, owners, quarter, step):
    half = owners // 2
    mine, plane, place = me // half, me // quarter, me % quarter
    group, turn = step // quarter, step % quarter
    if isinstance(step, int):
        plane_to = [(1 - mine) * 2, (1 - mine) * 2 + 1, mine * 2 + 1 - plane % 2, plane][group]
    else:
        plane_to = jnp.where(group < 2, (1 - mine) * 2 + group, jnp.where(group == 2, mine * 2 + 1 - plane % 2, plane))
    return plane_to * quarter + (place + turn + group // 3) % quarter


def exchange_kernel(
    owners, gate_up_ref, routes_ref, got_ref, raw_ref, named_ref, hidden_ref, send_ref, in_sem, send_sem, recv_sem
):
    me = lax.axis_index("expert")
    entries, _, width = gate_up_ref.shape
    picks, tok_rows = routes_ref.shape
    quarter = owners // 4
    pieces = in_sem.shape[0] - 1

    barrier = pltpu.get_barrier_semaphore()
    early = owners - quarter
    plane, place_in = me // quarter, me % quarter

    def greet(other):
        pl.semaphore_signal(barrier, inc=1, device_id={"expert": other}, device_id_type=MESH)

    @pl.when(plane < 3)
    def _():
        for turn in range(1, early):
            greet((me + turn) % early)

    @pl.when(plane == 3)
    def _():
        for turn in range(1, quarter):
            greet(early + (place_in + turn) % quarter)

    routes_in = pltpu.make_async_copy(routes_ref, named_ref, in_sem.at[pieces])
    routes_in.start()
    part = entries // pieces
    loads = []
    for piece in range(pieces):
        span = pl.ds(piece * part, part)
        loads.append(pltpu.make_async_copy(gate_up_ref.at[span], raw_ref.at[span], in_sem.at[piece]))
        loads[-1].start()

    routes_in.wait()
    token = lax.broadcasted_iota(jnp.int32, (tok_rows, entries), 0)
    entry = lax.broadcasted_iota(jnp.int32, (tok_rows, entries), 1)
    spread = (entry // picks == token).astype(jnp.float32)
    by_pick = jnp.dot(named_ref[...].astype(jnp.float32), spread, preferred_element_type=jnp.float32)
    pick = lax.broadcasted_iota(jnp.int32, (picks, entries), 0)
    entry = lax.broadcasted_iota(jnp.int32, (picks, entries), 1)
    flat = jnp.sum(jnp.where(entry % picks == pick, by_pick, 0.0), axis=0, keepdims=True).astype(jnp.int32)

    rows = owners * tok_rows
    row = lax.broadcasted_iota(jnp.int32, (rows, 1), 0)
    goes_to = partner(me, owners, quarter, row // tok_rows)
    entry = lax.broadcasted_iota(jnp.int32, (rows, entries), 1)
    choose = jnp.where((flat == goes_to) & (entry // picks == row % tok_rows), 1.0, 0.0).astype(jnp.bfloat16)

    for piece in range(pieces):
        loads[piece].wait()
        span = pl.ds(piece * part, part)
        both = raw_ref[span].reshape(part, 2 * width)
        gate = both[:, :width].astype(jnp.float32)
        upper = both[:, width:].astype(jnp.float32)
        hidden_ref[span] = (jax.nn.silu(gate) * upper).astype(jnp.bfloat16)

    def place(first, count):
        picked = choose[first : first + count]
        return jnp.dot(picked, hidden_ref[...], preferred_element_type=jnp.float32).astype(jnp.bfloat16)

    middle, last = rows // 2, rows - tok_rows
    send_ref[:middle] = place(0, middle)

    @pl.when(plane < 3)
    def _():
        pl.semaphore_wait(barrier, early - 1)
        for turn in range(quarter):
            greet(early + (place_in + turn) % quarter)

    @pl.when(plane == 3)
    def _():
        pl.semaphore_wait(barrier, owners - 1)
        for turn in range(early):
            greet(turn)

    parity = plane % 2

    def exchanged(step, slot):
        return pltpu.make_async_remote_copy(
            src_ref=send_ref.at[pl.ds(step * tok_rows, tok_rows)],
            dst_ref=got_ref.at[pl.ds(pl.multiple_of(slot * tok_rows, tok_rows), tok_rows)],
            send_sem=send_sem.at[step],
            recv_sem=recv_sem.at[slot],
            device_id={"expert": partner(me, owners, quarter, step)},
            device_id_type=MESH,
        )

    def send(step):
        slot = parity * quarter + step % quarter if step < owners // 2 else step
        exchanged(step, slot).start()

    def send_group(group):
        for step in range(group * quarter, min((group + 1) * quarter, owners - 1)):
            send(step)

    send_group(0)

    @pl.when(plane >= 2)
    def _():
        send_group(1)

    rest = place(middle, middle)
    send_ref[middle:] = rest[: last - middle]
    got_ref[last:, :] = rest[last - middle :]

    @pl.when(plane != 2)
    def _():
        send_group(2)

    send_group(3)

    @pl.when(plane < 3)
    def _():
        pl.semaphore_wait(barrier, quarter)

    @pl.when(plane < 2)
    def _():
        send_group(1)

    @pl.when(plane == 2)
    def _():
        send_group(2)

    for step in range(owners - 1):
        exchanged(step, step).wait()


def exchange(gate_up, routes, owners):
    entries, _, width = gate_up.shape
    picks, tok_rows = routes.shape
    rows = owners * tok_rows
    pieces = 4
    return pl.pallas_call(
        functools.partial(exchange_kernel, owners),
        out_shape=jax.ShapeDtypeStruct((rows, width), jnp.bfloat16),
        in_specs=[pl.BlockSpec(memory_space=pltpu.HBM)] * 2,
        out_specs=pl.BlockSpec(memory_space=pltpu.VMEM),
        scratch_shapes=[
            pltpu.VMEM((entries, 2, width), jnp.bfloat16),
            pltpu.VMEM((picks, tok_rows), jnp.int32),
            pltpu.VMEM((entries, width), jnp.bfloat16),
            pltpu.VMEM((rows - tok_rows, width), jnp.bfloat16),
            pltpu.SemaphoreType.DMA((pieces + 1,)),
            pltpu.SemaphoreType.DMA((owners - 1,)),
            pltpu.SemaphoreType.DMA((owners - 1,)),
        ],
        compiler_params=pltpu.CompilerParams(
            collective_id=0, has_side_effects=True, vmem_limit_bytes=32 * 1024 * 1024
        ),
    )(pltpu.with_memory_space_constraint(gate_up, pltpu.HBM), pltpu.with_memory_space_constraint(routes, pltpu.HBM))


def gram_kernel(scale, tiles, rows_ref, gram_ref, tile_ref, out_sem):
    width = rows_ref.shape[1]
    height = width // tiles
    writes = []
    for tile in range(tiles):
        span = pl.ds(tile * height, height)
        product = lax.dot_general(
            rows_ref[:, span], rows_ref[...], (((0,), (0,)), ((), ())), preferred_element_type=jnp.float32
        )
        tile_ref[span] = product * scale
        writes.append(pltpu.make_async_copy(tile_ref.at[span], gram_ref.at[span], out_sem.at[tile]))
        writes[-1].start()
    for write in writes:
        write.wait()


def gram_of(rows, scale):
    width = rows.shape[1]
    tiles = 8 if width % 1024 == 0 else 1
    return pl.pallas_call(
        functools.partial(gram_kernel, scale, tiles),
        out_shape=jax.ShapeDtypeStruct((width, width), jnp.float32),
        in_specs=[pl.BlockSpec(memory_space=pltpu.VMEM)],
        out_specs=pl.BlockSpec(memory_space=pltpu.HBM),
        scratch_shapes=[pltpu.VMEM((width, width), jnp.float32), pltpu.SemaphoreType.DMA((tiles,))],
        compiler_params=pltpu.CompilerParams(vmem_limit_bytes=32 * 1024 * 1024),
    )(rows)


def exchange_plain(hidden, routes, owners, capacity):
    entries, width = hidden.shape
    flat = routes.reshape(-1)
    onehot = (flat[:, None] == jnp.arange(owners, dtype=jnp.int32)[None, :]).astype(jnp.int32)
    ranks = jnp.sum(jnp.cumsum(onehot, axis=0) * onehot, axis=1) - 1
    slots = flat * capacity + ranks
    choose = (jnp.arange(owners * capacity, dtype=jnp.int32)[:, None] == slots[None, :]).astype(jnp.bfloat16)
    send = jnp.dot(choose, hidden, preferred_element_type=jnp.float32).astype(jnp.bfloat16)
    send = send.reshape(owners, capacity, width)
    return lax.all_to_all(send, "expert", split_axis=0, concat_axis=0, tiled=True).reshape(owners * capacity, width)


def per_device(gate_up, routes):
    tok_rows, picks, _, width = gate_up.shape
    owners = lax.axis_size("expert")
    halves = lax.axis_size("sub")
    capacity = max(2, min(tok_rows, 2 * tok_rows * picks // owners))
    scale = 1.0 / (tok_rows * picks * halves)
    if capacity == tok_rows and tok_rows % 16 == 0 and owners % 4 == 0 and owners <= 32 and halves == 1:
        rows = exchange(gate_up.reshape(tok_rows * picks, 2, width), routes.T, owners)
        return gram_of(rows, scale)[None]
    hidden = hidden_rows(gate_up).reshape(tok_rows * picks, width)
    rows = exchange_plain(hidden, routes, owners, capacity)
    gram = jnp.einsum("rc,rd->cd", rows, rows, preferred_element_type=jnp.float32)
    gram = lax.psum_scatter(gram, "sub", scatter_dimension=0, tiled=True)
    return (gram * scale)[None]


def solution(mesh):
    placed = (
        P(("groups", "expert", "sub"), None, None, None),
        P(("groups", "expert", "sub"), None),
    )
    return jax.shard_map(
        per_device,
        mesh=mesh,
        in_specs=placed,
        out_specs=P(("groups", "expert"), "sub", None),
        check_vma=False,
    )
```
